32 devices in a mesh: dp: 16 (over z, y, core), proto: 2 (over x).
Axes of the slice: x: 2, y: 2, z: 4, core: 2. Of those that a mesh axis runs over, the one named last changes fastest.
Arguments:
- feature_matrix: bfloat16 [4096, 128], P('dp'), may hold values from -64 to 64
- tangent_embed: bfloat16 [4096, 128], P('dp'), may hold values from -2 to 2
- anchor_matrix: bfloat16 [65536, 128], P('proto'), may hold values from -4 to 4
- anchor_perturbation: bfloat16 [65536, 128], P('proto'), may hold values from -0.5 to 0.5
- codes: bfloat16 [4096, 65536], P('dp', 'proto'), may hold values from 0 to 3, as said below
- partner_lookup: int32 [4096], P('dp'), may hold values from 0 to 4095, as said below
Outputs:
- hvp_embed: bfloat16 [4096, 128], P('dp')
- hvp_proto: bfloat16 [65536, 128], P('proto')
The draws below stay inside these ranges and needn't reach their ends.
Inputs may be any that keep to these rules, and one draw needn't show every extreme that they name: partner_lookup[partner_lookup[i]] = i and partner_lookup[i] != i for every crop i. `codes`: positive.
All inputs are finite; a program needn't handle non-finite values.
Results may differ from the reference program's by a relative error of at most 0.0051.
Values may be sent and summed in bfloat16 or wider, within the bound.
A program may use at most 192 MiB of HBM per device.

```python
import math
import jax
import jax.numpy as jnp
from jax import lax

D = 128
PROTOS = 65536
CROPS = 4096


def embed_pair(key):
    keys = jax.random.split(jax.random.fold_in(key, 7), 6)
    row_scale = jnp.exp(jax.random.uniform(keys[0], (CROPS, 1), jnp.float32, math.log(0.1), 0.0))
    col_scale = jnp.exp(jax.random.uniform(keys[1], (PROTOS, 1), jnp.float32, math.log(0.3), math.log(3.0)))
    raw_rows = jnp.clip(jax.random.normal(keys[4], (CROPS, D), jnp.float32), -6.0, 6.0)
    raw_cols = jnp.clip(jax.random.normal(keys[5], (PROTOS, D), jnp.float32), -6.0, 6.0)
    embed_values = row_scale * raw_rows
    proto_values = col_scale * raw_cols / math.sqrt(D)
    return (embed_values, proto_values)


def draw_feature_matrix(key, part):
    return embed_pair(key)[0].astype(jnp.bfloat16)


def draw_anchor_matrix(key, part):
    return embed_pair(key)[1].astype(jnp.bfloat16)


def draw_tangent_embed(key, part):
    keys = jax.random.split(jax.random.fold_in(key, 17), 3)
    values = jnp.clip(0.3 * jax.random.normal(keys[2], (CROPS, D), jnp.float32), -2.0, 2.0)
    return values.astype(jnp.bfloat16)


def draw_codes(key, part):
    keys = jax.random.split(jax.random.fold_in(key, 11), 2)
    raw = jnp.clip(jax.random.normal(keys[0], (CROPS, PROTOS), jnp.float32), -5.0, 5.0)
    row_factor = jnp.exp(jax.random.uniform(keys[1], (CROPS, 1), jnp.float32, math.log(0.3), math.log(3.0)))
    position = jnp.arange(PROTOS, dtype=jnp.float32)[None, :] / PROTOS
    trend = jnp.exp(math.log(3.0) * position)
    values = jnp.exp(0.5 * raw - 0.125) * row_factor * trend / PROTOS
    return values.astype(jnp.bfloat16)


def draw_partner_lookup(key, part):
    order = jax.random.permutation(jax.random.fold_in(key, 13), CROPS).astype(jnp.int32)
    partner = order.reshape(-1, 2)[:, ::-1].reshape(-1)
    return jnp.zeros((CROPS,), jnp.int32).at[order].set(partner)


def level_of(own_key, dims, shards, least, high):
    level, own = 1.0, jax.random.fold_in(own_key, 6)
    for dim, shards_of in shards:
        steps = jnp.exp(jax.random.uniform(jax.random.fold_in(own, dim), (shards_of,), jnp.float32, least / len(shards), high / len(shards)))
        level = level * jnp.repeat(steps, dims[dim] // shards_of).reshape([-1 if axis == dim else 1 for axis in range(len(dims))])
    return level


def centred(stream_key, extent, width, limit, cuts=(), held_as=jnp.bfloat16):
    values = jax.random.normal(stream_key, extent, jnp.float32) * width
    if len(cuts) > 0:
        values = level_of(stream_key, extent, cuts, -0.22, 0.18) * values
    return jnp.clip(values, min=-limit, max=limit).astype(held_as)


def setup_inputs(seed: int = 0) -> dict:
    splits = jax.random.split(jax.random.key(seed), 7)
    return {
        "feature_matrix": draw_feature_matrix(jax.random.fold_in(splits[6], 71), 0),
        "tangent_embed": draw_tangent_embed(jax.random.fold_in(splits[6], 71), 0),
        "anchor_matrix": draw_anchor_matrix(jax.random.fold_in(splits[6], 71), 0),
        "anchor_perturbation": centred(splits[3], (PROTOS, D), D ** -0.5, 0.5, ((0, 2),)),
        "codes": draw_codes(jax.random.fold_in(splits[6], 71), 0),
        "partner_lookup": draw_partner_lookup(jax.random.fold_in(splits[6], 71), 0),
    }


softening_constant = 0.1


def aggregated_elements(left, right):
    return lax.dot_general(left, right, (((1,), (1,)), ((), ())), preferred_element_type=jnp.float32)


def reduce_along_samples(left, right):
    return lax.dot_general(left, right, (((0,), (0,)), ((), ())), preferred_element_type=jnp.float32)


def reference(feature_matrix, tangent_embed, anchor_matrix, anchor_perturbation, codes, partner_lookup):
    traded_contributions = jnp.take(feature_matrix, partner_lookup, axis=0)
    swapped_tan = jnp.take(tangent_embed, partner_lookup, axis=0)
    tile_height = math.gcd(CROPS, 256)

    def one_block(running, block_index):
        sample_offset = (block_index * tile_height).astype(jnp.int32)
        traded_portion = lax.dynamic_slice_in_dim(traded_contributions, sample_offset, tile_height, 0)
        direction_piece = lax.dynamic_slice_in_dim(swapped_tan, sample_offset, tile_height, 0)
        code_piece = lax.dynamic_slice_in_dim(codes, sample_offset, tile_height, 0)
        unscaled_affinity = aggregated_elements(traded_portion, anchor_matrix) / softening_constant
        similarity_direction = (aggregated_elements(direction_piece, anchor_matrix) + aggregated_elements(traded_portion, anchor_perturbation)) / softening_constant
        highest = jnp.max(unscaled_affinity, axis=1, keepdims=True)
        exponent = jnp.exp(unscaled_affinity - highest)
        softmax_total = jnp.sum(exponent, axis=1, keepdims=True)
        weighted = jnp.sum(exponent * similarity_direction, axis=1, keepdims=True)
        line_sum_norm = jnp.sum(code_piece.astype(jnp.float32), axis=1, keepdims=True)
        model_likelihood = exponent / softmax_total
        mean_code_vector = weighted / softmax_total
        outer_patch_multiplier = (softening_constant * line_sum_norm * model_likelihood * (similarity_direction - mean_code_vector)).astype(jnp.bfloat16)
        right_crop_factor = (softening_constant * (line_sum_norm * model_likelihood - code_piece.astype(jnp.float32))).astype(jnp.bfloat16)
        hvp_rows = jnp.dot(outer_patch_multiplier, anchor_matrix, preferred_element_type=jnp.float32) + jnp.dot(right_crop_factor, anchor_perturbation, preferred_element_type=jnp.float32)
        running = running + reduce_along_samples(outer_patch_multiplier, traded_portion) + reduce_along_samples(right_crop_factor, direction_piece)
        return running, hvp_rows

    proto_sum, hvp_blocks = lax.scan(one_block, jnp.zeros((PROTOS, D), jnp.float32), jnp.arange(CROPS // tile_height, dtype=jnp.int32))
    hvp_swapped = hvp_blocks.reshape(CROPS, D).astype(jnp.bfloat16)
    return jnp.take(hvp_swapped, partner_lookup, axis=0), proto_sum.astype(jnp.bfloat16)
```

```python
import functools
import math

import jax
import jax.numpy as jnp
from jax import lax
from jax.experimental import pallas as pl
from jax.experimental.pallas import tpu as pltpu
from jax.sharding import PartitionSpec as P

MESH = pl.DeviceIdType.MESH
F32 = jnp.float32
BF16 = jnp.bfloat16
LOG2E = math.log2(math.e)
TEMP = 0.1
SCALE = LOG2E / TEMP
LANES = 128
MIB = 1024 * 1024


def place(n):
    d = lax.axis_index("dp")
    return d // 4, (d // 2) % 2, d % 2, n // 4


def index_of(a, b, c):
    return (a * 2 + b) * 2 + c


def greet(a, b, c, length):
    barrier = pltpu.get_barrier_semaphore()

    def hello(target):
        pl.semaphore_signal(barrier, inc=1, device_id={"dp": target}, device_id_type=MESH)

    hello(index_of(a, b, 1 - c))
    hello(index_of(a, 1 - b, c))

    @pl.when(a > 0)
    def _():
        hello(index_of(a - 1, b, c))

    @pl.when(a < length - 1)
    def _():
        hello(index_of(a + 1, b, c))

    peers = 2 + jnp.where(a > 0, 1, 0) + jnp.where(a < length - 1, 1, 0)
    pl.semaphore_wait(barrier, peers)


class Copies:
    def __init__(self, arrays, block, kind, target):
        self.copies = [
            pltpu.make_async_remote_copy(
                src_ref=out.at[block],
                dst_ref=out.at[block],
                send_sem=send.at[kind, block],
                recv_sem=recv.at[block],
                device_id={"dp": target},
                device_id_type=MESH,
            )
            for out, send, recv in arrays
        ]

    def start(self):
        for copy in self.copies:
            copy.start()

    def wait_send(self):
        for copy in self.copies:
            copy.wait_send()

    def wait_recv(self):
        for copy in self.copies:
            copy.wait_recv()


def gather_steps(arrays, a, b, c, length):
    def copy(block, kind, target):
        return Copies(arrays, block, kind, target)

    right, left = index_of(a + 1, b, c), index_of(a - 1, b, c)
    pair, twin = index_of(a, 1 - b, c), index_of(a, b, 1 - c)

    def line_block(pos):
        return index_of(pos, b, c)

    def spread(block, to_right, to_left):
        if to_right:

            @pl.when(a < length - 1)
            def _():
                copy(block, 0, right).start()

        if to_left:

            @pl.when(a > 0)
            def _():
                copy(block, 1, left).start()

        copy(block, 2, pair).start()
        copy(block, 3, twin).start()

    def from_pair(pos):
        block = index_of(pos, 1 - b, c)
        copy(block, 2, pair).wait_recv()
        copy(block, 3, twin).start()

    spread(line_block(a), True, True)
    for k in range(1, length):

        @pl.when(a - k >= 0)
        def _():
            copy(line_block(a - k), 0, right).wait_recv()
            spread(line_block(a - k), True, False)

        @pl.when(a + k < length)
        def _():
            copy(line_block(a + k), 1, left).wait_recv()
            spread(line_block(a + k), False, True)

    from_pair(a)
    for k in range(1, length):

        @pl.when(a - k >= 0)
        def _():
            from_pair(a - k)

        @pl.when(a + k < length)
        def _():
            from_pair(a + k)

    for pos in range(length):
        for side in range(2):
            copy(index_of(pos, side, 1 - c), 3, twin).wait_recv()
    for pos in range(length):
        copy(line_block(pos), 2, pair).wait_send()
        for side in range(2):
            copy(index_of(pos, side, c), 3, twin).wait_send()

        @pl.when(jnp.logical_and(a < length - 1, pos <= a))
        def _():
            copy(line_block(pos), 0, right).wait_send()

        @pl.when(jnp.logical_and(a > 0, pos >= a))
        def _():
            copy(line_block(pos), 1, left).wait_send()


def gather_kernel(n, x, out, send, recv, local):
    a, b, c, length = place(n)
    own = pltpu.make_async_copy(x, out.at[index_of(a, b, c)], local)
    own.start()
    greet(a, b, c, length)
    own.wait()
    gather_steps([(out, send, recv)], a, b, c, length)


def gather_call(n, x, collective_id):
    return pl.pallas_call(
        functools.partial(gather_kernel, n),
        out_shape=jax.ShapeDtypeStruct((n,) + x.shape, x.dtype),
        in_specs=[pl.BlockSpec(memory_space=pltpu.VMEM)],
        out_specs=pl.BlockSpec(memory_space=pltpu.VMEM),
        scratch_shapes=[
            pltpu.SemaphoreType.DMA((4, n)),
            pltpu.SemaphoreType.DMA((n,)),
            pltpu.SemaphoreType.DMA,
        ],
        compiler_params=pltpu.CompilerParams(
            collective_id=collective_id, has_side_effects=True, vmem_limit_bytes=32 * MIB
        ),
    )(x)


def reduce_kernel(n, parts, embed, out, embeds, own1, recv1, recv2, recv_l, recv_r, out2, out_l, out_r,
                  load, s1, r1, s2, r2, sl, sr, rl, rr, local, g_send, g_recv, e_send, e_recv):
    a, b, c, length = place(n)
    rows = parts.shape[1]
    step = 256
    right, left = index_of(a + 1, b, c), index_of(a - 1, b, c)
    pair, twin = index_of(a, 1 - b, c), index_of(a, b, 1 - c)
    embed_in = pltpu.make_async_copy(embed, embeds.at[index_of(a, b, c)], local.at[0])
    embed_in.start()

    def order(j):
        return jnp.where(a < length // 2, (a - 1 - j + 2 * length) % length, (a + 1 + j) % length)

    def remote(src, dst, send, recv, target):
        return pltpu.make_async_remote_copy(
            src_ref=src, dst_ref=dst, send_sem=send, recv_sem=recv, device_id={"dp": target}, device_id_type=MESH
        )

    def to_twin(pos, side):
        k = pos * 2 + side
        return remote(parts.at[index_of(pos, side, 1 - c)], recv1.at[k], s1.at[k], r1.at[k], twin)

    def load_own(pos, side):
        k = pos * 2 + side
        return pltpu.make_async_copy(parts.at[index_of(pos, side, c)], own1.at[k], load.at[k])

    def to_pair(pos):
        return remote(out2.at[pos], recv2.at[pos], s2.at[pos], r2.at[pos], pair)

    def to_right(pos):
        return remote(out_r.at[pos], recv_l.at[pos], sr.at[pos], rl.at[pos], right)

    def to_left(pos):
        return remote(out_l.at[pos], recv_r.at[pos], sl.at[pos], rr.at[pos], left)

    for j in range(length):
        for side in (1 - b, b):
            load_own(order(j), side).start()
    greet(a, b, c, length)
    for side in (1 - b, b):
        for j in range(length):
            to_twin(order(j), side).start()
    embed_in.wait()

    def added(dst, srcs):
        def one(i, carry):
            at = pl.ds(pl.multiple_of(i * step, step), step)
            total = srcs[0][at, :].astype(F32)
            for src in srcs[1:]:
                total = total + src[at, :].astype(F32)
            dst[at, :] = total.astype(dst.dtype)
            return carry

        lax.fori_loop(0, rows // step, one, 0)

    for j in range(length):
        pos = order(j)
        k = pos * 2 + 1 - b
        load_own(pos, 1 - b).wait()
        to_twin(pos, 1 - b).wait_recv()
        added(out2.at[pos], [own1.at[k], recv1.at[k]])
        to_pair(pos).start()

    for j in range(length):
        load_own(order(j), b).wait()
        to_twin(order(j), b).wait_recv()

    def terms(pos):
        k = pos * 2 + b
        return [own1.at[k], recv1.at[k], recv2.at[pos]]

    for t in range(length - 1):
        r_pos = length - 1 - (t - a)
        l_pos = t - (length - 1 - a)

        @pl.when(jnp.logical_and(t - a >= 0, r_pos > a))
        def _():
            to_pair(r_pos).wait_recv()

            @pl.when(a > 0)
            def _():
                to_right(r_pos).wait_recv()
                added(out_r.at[r_pos], terms(r_pos) + [recv_l.at[r_pos]])

            @pl.when(a == 0)
            def _():
                added(out_r.at[r_pos], terms(r_pos))

            to_right(r_pos).start()

        @pl.when(jnp.logical_and(l_pos >= 0, l_pos < a))
        def _():
            to_pair(l_pos).wait_recv()

            @pl.when(a < length - 1)
            def _():
                to_left(l_pos).wait_recv()
                added(out_l.at[l_pos], terms(l_pos) + [recv_r.at[l_pos]])

            @pl.when(a == length - 1)
            def _():
                added(out_l.at[l_pos], terms(l_pos))

            to_left(l_pos).start()

    to_pair(a).wait_recv()
    final = own1.at[a * 2 + b]

    @pl.when(a > 0)
    def _():
        to_right(a).wait_recv()

    @pl.when(a < length - 1)
    def _():
        to_left(a).wait_recv()

    @pl.when(a == 0)
    def _():
        added(final, terms(a) + [recv_r.at[a]])

    @pl.when(a == length - 1)
    def _():
        added(final, terms(a) + [recv_l.at[a]])

    @pl.when(jnp.logical_and(a > 0, a < length - 1))
    def _():
        added(final, terms(a) + [recv_l.at[a], recv_r.at[a]])

    done = pltpu.make_async_copy(final, out.at[index_of(a, b, c)], local.at[1])
    done.start()
    done.wait()
    gather_steps([(embeds, e_send, e_recv), (out, g_send, g_recv)], a, b, c, length)

    for pos in range(length):
        for side in range(2):
            to_twin(pos, side).wait_send()
        to_pair(pos).wait_send()

        @pl.when(pos > a)
        def _():
            to_right(pos).wait_send()

        @pl.when(pos < a)
        def _():
            to_left(pos).wait_send()


def reduce_call(n, parts, embed, collective_id):
    length = n // 4
    rows, width = parts.shape[1:]
    sems = pltpu.SemaphoreType.DMA
    block = lambda count: pltpu.VMEM((count, rows, width), BF16)
    return pl.pallas_call(
        functools.partial(reduce_kernel, n),
        out_shape=(
            jax.ShapeDtypeStruct(parts.shape, BF16),
            jax.ShapeDtypeStruct((n,) + embed.shape, BF16),
        ),
        in_specs=[pl.BlockSpec(memory_space=pl.ANY)] * 2,
        out_specs=[pl.BlockSpec(memory_space=pl.ANY)] * 2,
        scratch_shapes=[
            block(2 * length), block(2 * length), block(length), block(length), block(length),
            block(length), block(length), block(length),
            sems((2 * length,)), sems((2 * length,)), sems((2 * length,)), sems((length,)), sems((length,)),
            sems((length,)), sems((length,)), sems((length,)), sems((length,)), sems((2,)),
            sems((4, n)), sems((n,)), sems((4, n)), sems((n,)),
        ],
        compiler_params=pltpu.CompilerParams(
            collective_id=collective_id, has_side_effects=True, vmem_limit_bytes=48 * MIB
        ),
    )(parts, embed)


def dot_t(left, right):
    return lax.dot_general(left, right, (((1,), (1,)), ((), ())), preferred_element_type=F32)


def stats_kernel(rows_ref, tans_ref, a_ref, b_ref, codes_ref, out_ref, top, total, weighted, mass):
    i = pl.program_id(0)
    chunk = a_ref.shape[0]

    @pl.when(i == 0)
    def _():
        top[...] = jnp.full_like(top, -1e30)
        total[...] = jnp.zeros_like(total)
        weighted[...] = jnp.zeros_like(weighted)
        mass[...] = jnp.zeros_like(mass)

    s = dot_t(rows_ref[...], a_ref[...])
    pairs = jnp.concatenate([a_ref[...], b_ref[...]], axis=1)
    tan = dot_t(jnp.concatenate([tans_ref[...], rows_ref[...]], axis=1), pairs)
    cols = [slice(k, k + LANES) for k in range(0, chunk, LANES)]
    old = top[...]
    new = functools.reduce(jnp.maximum, [s[:, k] for k in cols], old)
    fade = jnp.exp2((old - new) * SCALE)
    z, w, q = total[...] * fade, weighted[...] * fade, mass[...]
    for k in cols:
        e = jnp.exp2((s[:, k] - new) * SCALE)
        z = z + e
        w = w + e * tan[:, k]
        q = q + codes_ref[:, k].astype(F32)
    top[...], total[...], weighted[...], mass[...] = new, z, w, q

    @pl.when(i == pl.num_programs(0) - 1)
    def _():
        peak = jnp.max(top[...], axis=1, keepdims=True)
        scale = jnp.exp2((top[...] - peak) * SCALE)
        lane = lax.broadcasted_iota(jnp.int32, out_ref.shape, 1)
        values = [
            peak,
            jnp.sum(total[...] * scale, axis=1, keepdims=True),
            jnp.sum(weighted[...] * scale, axis=1, keepdims=True),
            jnp.sum(mass[...], axis=1, keepdims=True),
        ]
        out = jnp.zeros(out_ref.shape, F32)
        for k, v in enumerate(values):
            out = jnp.where(lane == k, v, out)
        out_ref[...] = out


def stats_call(rows, tans, anchors, moves, codes):
    crops, width = rows.shape
    protos = anchors.shape[0]
    chunk = math.gcd(protos, 1024)
    whole = pl.BlockSpec((crops, width), lambda i: (0, 0))
    block = pl.BlockSpec((chunk, width), lambda i: (i, 0))
    return pl.pallas_call(
        stats_kernel,
        grid=(protos // chunk,),
        out_shape=jax.ShapeDtypeStruct((crops, LANES), F32),
        in_specs=[whole, whole, block, block, pl.BlockSpec((crops, chunk), lambda i: (0, i))],
        out_specs=pl.BlockSpec((crops, LANES), lambda i: (0, 0)),
        scratch_shapes=[pltpu.VMEM((crops, LANES), F32)] * 4,
        compiler_params=pltpu.CompilerParams(vmem_limit_bytes=40 * MIB),
    )(rows, tans, anchors, moves, codes)


def weights_kernel(rows_ref, tans_ref, a_ref, b_ref, codes_ref, stats_ref, part_ref, embed_ref):
    i = pl.program_id(0)

    @pl.when(i == 0)
    def _():
        embed_ref[...] = jnp.zeros_like(embed_ref)

    s = dot_t(rows_ref[...], a_ref[...])
    pairs = jnp.concatenate([a_ref[...], b_ref[...]], axis=1)
    tan = dot_t(jnp.concatenate([tans_ref[...], rows_ref[...]], axis=1), pairs)
    peak, gain, mean = stats_ref[:, 0:1], stats_ref[:, 1:2], stats_ref[:, 2:3]
    p = jnp.exp2((s - peak) * SCALE) * gain
    u = (p * (tan - mean)).astype(BF16)
    v = (TEMP * (p - codes_ref[...].astype(F32))).astype(BF16)
    embed_ref[...] += jnp.dot(u, a_ref[...], preferred_element_type=F32) + jnp.dot(
        v, b_ref[...], preferred_element_type=F32
    )
    both = jnp.concatenate([u, v], axis=0)
    ends = jnp.concatenate([rows_ref[...], tans_ref[...]], axis=0)
    part_ref[...] = lax.dot_general(
        both, ends, (((0,), (0,)), ((), ())), preferred_element_type=F32
    ).astype(BF16)


def weights_call(rows, tans, anchors, moves, codes, stats):
    crops, width = rows.shape
    protos = anchors.shape[0]
    chunk = math.gcd(protos, 1024)
    whole = pl.BlockSpec((crops, width), lambda i: (0, 0))
    block = pl.BlockSpec((chunk, width), lambda i: (i, 0))
    return pl.pallas_call(
        weights_kernel,
        grid=(protos // chunk,),
        out_shape=(
            jax.ShapeDtypeStruct((protos, width), BF16),
            jax.ShapeDtypeStruct((crops, width), F32),
        ),
        in_specs=[
            whole, whole, block, block,
            pl.BlockSpec((crops, chunk), lambda i: (0, i)),
            pl.BlockSpec((crops, LANES), lambda i: (0, 0)),
        ],
        out_specs=(block, whole),
        compiler_params=pltpu.CompilerParams(vmem_limit_bytes=40 * MIB),
    )(rows, tans, anchors, moves, codes, stats)


def body(n, n_proto, features, tangents, anchors, moves, codes, partner):
    crops, width = features.shape
    gathered = gather_call(n, jnp.concatenate([features, tangents], axis=1), 1)
    swapped = jnp.take(gathered.reshape(n * crops, 2 * width), partner, axis=0)
    rows, tans = swapped[:, :width], swapped[:, width:]
    local = stats_call(rows, tans, anchors, moves, codes)[:, :4].T
    mine = jnp.arange(n_proto) == lax.axis_index("proto")
    every = lax.psum(jnp.where(mine[:, None, None], local[None], 0.0), "proto")
    peak = jnp.max(every[:, 0], axis=0)
    scale = jnp.exp2((every[:, 0] - peak) * SCALE)
    total = jnp.sum(every[:, 1] * scale, axis=0)
    mean = jnp.sum(every[:, 2] * scale, axis=0) / total
    mass = jnp.sum(every[:, 3], axis=0)
    stats = jnp.stack([peak, mass / total, mean], axis=1)
    stats = jnp.pad(stats, ((0, 0), (0, LANES - 3)))
    parts, embed = weights_call(rows, tans, anchors, moves, codes, stats)
    embed = lax.psum(embed, "proto").astype(BF16)
    protos = anchors.shape[0]
    out, embeds = reduce_call(n, parts.reshape(n, protos // n, width), embed, 2)
    hvp_embed = jnp.take(embeds.reshape(n * crops, width), partner, axis=0)
    return hvp_embed, out.reshape(protos, width)


def solution(mesh):
    in_specs = (
        P("dp", None),
        P("dp", None),
        P("proto", None),
        P("proto", None),
        P("dp", "proto"),
        P("dp"),
    )
    out_specs = (P("dp", None), P("proto", None))
    return jax.shard_map(
        functools.partial(body, mesh.shape["dp"], mesh.shape["proto"]),
        mesh=mesh,
        in_specs=in_specs,
        out_specs=out_specs,
        check_vma=False,
    )
```

```python
import functools
import math

import jax
import jax.numpy as jnp
from jax import lax
from jax.experimental import pallas as pl
from jax.experimental.pallas import tpu as pltpu
from jax.sharding import PartitionSpec as P

MESH = pl.DeviceIdType.MESH
F32 = jnp.float32
BF16 = jnp.bfloat16
LOG2E = math.log2(math.e)
TEMP = 0.1
SCALE = LOG2E / TEMP
LANES = 128
MIB = 1024 * 1024


def place(n):
    d = lax.axis_index("dp")
    return d // 4, (d // 2) % 2, d % 2, n // 4


def index_of(a, b, c):
    return (a * 2 + b) * 2 + c


def greet(a, b, c, length, n_proto=1):
    barrier = pltpu.get_barrier_semaphore()

    def hello(target):
        pl.semaphore_signal(barrier, inc=1, device_id={"dp": target}, device_id_type=MESH)

    hello(index_of(a, b, 1 - c))
    hello(index_of(a, 1 - b, c))

    @pl.when(a > 0)
    def _():
        hello(index_of(a - 1, b, c))

    @pl.when(a < length - 1)
    def _():
        hello(index_of(a + 1, b, c))

    me = lax.axis_index("proto")
    for k in range(1, n_proto):
        pl.semaphore_signal(barrier, inc=1, device_id={"proto": (me + k) % n_proto}, device_id_type=MESH)
    peers = 1 + n_proto + jnp.where(a > 0, 1, 0) + jnp.where(a < length - 1, 1, 0)
    pl.semaphore_wait(barrier, peers)


class Copies:
    def __init__(self, arrays, block, kind, target):
        self.copies = [
            pltpu.make_async_remote_copy(
                src_ref=out.at[block],
                dst_ref=out.at[block],
                send_sem=send.at[kind, block],
                recv_sem=recv.at[block],
                device_id={"dp": target},
                device_id_type=MESH,
            )
            for out, send, recv in arrays
        ]

    def start(self):
        for copy in self.copies:
            copy.start()

    def wait_send(self):
        for copy in self.copies:
            copy.wait_send()

    def wait_recv(self):
        for copy in self.copies:
            copy.wait_recv()


def gather_steps(arrays, a, b, c, length):
    def copy(block, kind, target):
        return Copies(arrays, block, kind, target)

    right, left = index_of(a + 1, b, c), index_of(a - 1, b, c)
    pair, twin = index_of(a, 1 - b, c), index_of(a, b, 1 - c)

    def line_block(pos):
        return index_of(pos, b, c)

    def spread(block, to_right, to_left):
        if to_right:

            @pl.when(a < length - 1)
            def _():
                copy(block, 0, right).start()

        if to_left:

            @pl.when(a > 0)
            def _():
                copy(block, 1, left).start()

        copy(block, 2, pair).start()
        copy(block, 3, twin).start()

    def from_pair(pos):
        block = index_of(pos, 1 - b, c)
        copy(block, 2, pair).wait_recv()
        copy(block, 3, twin).start()

    spread(line_block(a), True, True)
    for k in range(1, length):

        @pl.when(a - k >= 0)
        def _():
            copy(line_block(a - k), 0, right).wait_recv()
            spread(line_block(a - k), True, False)

        @pl.when(a + k < length)
        def _():
            copy(line_block(a + k), 1, left).wait_recv()
            spread(line_block(a + k), False, True)

    from_pair(a)
    for k in range(1, length):

        @pl.when(a - k >= 0)
        def _():
            from_pair(a - k)

        @pl.when(a + k < length)
        def _():
            from_pair(a + k)

    for pos in range(length):
        for side in range(2):
            copy(index_of(pos, side, 1 - c), 3, twin).wait_recv()
    for pos in range(length):
        copy(line_block(pos), 2, pair).wait_send()
        for side in range(2):
            copy(index_of(pos, side, c), 3, twin).wait_send()

        @pl.when(jnp.logical_and(a < length - 1, pos <= a))
        def _():
            copy(line_block(pos), 0, right).wait_send()

        @pl.when(jnp.logical_and(a > 0, pos >= a))
        def _():
            copy(line_block(pos), 1, left).wait_send()


def gather_kernel(n, x, out, send, recv, local):
    a, b, c, length = place(n)
    own = pltpu.make_async_copy(x, out.at[index_of(a, b, c)], local)
    own.start()
    greet(a, b, c, length)
    own.wait()
    gather_steps([(out, send, recv)], a, b, c, length)


def gather_call(n, x, collective_id):
    return pl.pallas_call(
        functools.partial(gather_kernel, n),
        out_shape=jax.ShapeDtypeStruct((n,) + x.shape, x.dtype),
        in_specs=[pl.BlockSpec(memory_space=pltpu.VMEM)],
        out_specs=pl.BlockSpec(memory_space=pltpu.VMEM),
        scratch_shapes=[
            pltpu.SemaphoreType.DMA((4, n)),
            pltpu.SemaphoreType.DMA((n,)),
            pltpu.SemaphoreType.DMA,
        ],
        compiler_params=pltpu.CompilerParams(
            collective_id=collective_id, has_side_effects=True, vmem_limit_bytes=56 * MIB
        ),
    )(x)


def reduce_kernel(n, n_proto, rows_ref, tans_ref, stats_ref, anchors, moves, codes, out, embeds,
                  a_buf, b_buf, c_buf, parts, recv1, recv2, recv_l, recv_r, out2, out_l, out_r, embed_sum, embed_in,
                  load, s1, r1, s2, r2, sl, sr, rl, rr, sx, rx, local, g_send, g_recv, e_send, e_recv):
    a, b, c, length = place(n)
    me = lax.axis_index("proto")
    rows = parts.shape[1]
    step = math.gcd(rows, 256)
    tile = math.gcd(rows, 1024)
    tiles = rows // tile
    right, left = index_of(a + 1, b, c), index_of(a - 1, b, c)
    pair, twin = index_of(a, 1 - b, c), index_of(a, b, 1 - c)

    def order(j):
        return jnp.where(a < length // 2, (a - 1 - j + 2 * length) % length, (a + 1 + j) % length)

    def remote(src, dst, send, recv, target):
        return pltpu.make_async_remote_copy(
            src_ref=src, dst_ref=dst, send_sem=send, recv_sem=recv, device_id={"dp": target}, device_id_type=MESH
        )

    def to_twin(pos, side):
        k = pos * 2 + side
        return remote(parts.at[k * 2], recv1.at[k], s1.at[k], r1.at[k], twin)

    def own_part(pos, side):
        return parts.at[(pos * 2 + side) * 2 + 1]

    def to_peer(k):
        return pltpu.make_async_remote_copy(
            src_ref=embed_sum,
            dst_ref=embed_in.at[me],
            send_sem=sx.at[k],
            recv_sem=rx.at[k],
            device_id={"proto": (me + k) % n_proto},
            device_id_type=MESH,
        )

    def fetches(q, pos, side):
        slot = q % 2
        copies = []
        for w, core in enumerate((1 - c, c)):
            at = pl.ds(pl.multiple_of(index_of(pos, side, core) * rows, rows), rows)
            copies += [
                pltpu.make_async_copy(anchors.at[at, :], a_buf.at[slot, w], load.at[slot, w, 0]),
                pltpu.make_async_copy(moves.at[at, :], b_buf.at[slot, w], load.at[slot, w, 1]),
                pltpu.make_async_copy(codes.at[:, at], c_buf.at[slot, w], load.at[slot, w, 2]),
            ]
        return copies

    def make(q, pos, side):
        slot = q % 2

        def one(i, carry):
            w, at = i // tiles, pl.ds(pl.multiple_of((i % tiles) * tile, tile), tile)
            anchor, move, code = a_buf[slot, w, at, :], b_buf[slot, w, at, :], c_buf[slot, w, :, at]
            part, embed = weights(rows_ref[...], tans_ref[...], anchor, move, code, stats_ref)
            parts[(pos * 2 + side) * 2 + w, at, :] = part
            embed_sum[...] += embed
            return carry

        lax.fori_loop(0, 2 * tiles, one, 0)

    def to_pair(pos):
        return remote(out2.at[pos], recv2.at[pos], s2.at[pos], r2.at[pos], pair)

    def to_right(pos):
        return remote(out_r.at[pos], recv_l.at[pos], sr.at[pos], rl.at[pos], right)

    def to_left(pos):
        return remote(out_l.at[pos], recv_r.at[pos], sl.at[pos], rr.at[pos], left)

    def added(dst, srcs):
        def one(i, carry):
            at = pl.ds(pl.multiple_of(i * step, step), step)
            total = srcs[0][at, :].astype(F32)
            for src in srcs[1:]:
                total = total + src[at, :].astype(F32)
            dst[at, :] = total.astype(dst.dtype)
            return carry

        lax.fori_loop(0, rows // step, one, 0)

    def terms(pos):
        return [own_part(pos, b), recv1.at[pos * 2 + b], recv2.at[pos]]

    def to_line(t):
        r_pos = length - 1 - (t - a)
        l_pos = t - (length - 1 - a)

        @pl.when(jnp.logical_and(t - a >= 0, r_pos > a))
        def _():
            to_pair(r_pos).wait_recv()

            @pl.when(a > 0)
            def _():
                to_right(r_pos).wait_recv()
                added(out_r.at[r_pos], terms(r_pos) + [recv_l.at[r_pos]])

            @pl.when(a == 0)
            def _():
                added(out_r.at[r_pos], terms(r_pos))

            to_right(r_pos).start()

        @pl.when(jnp.logical_and(l_pos >= 0, l_pos < a))
        def _():
            to_pair(l_pos).wait_recv()

            @pl.when(a < length - 1)
            def _():
                to_left(l_pos).wait_recv()
                added(out_l.at[l_pos], terms(l_pos) + [recv_r.at[l_pos]])

            @pl.when(a == length - 1)
            def _():
                added(out_l.at[l_pos], terms(l_pos))

            to_left(l_pos).start()

    def received(j, crossing):
        pos = order(j)
        side = 1 - b if crossing else b
        to_twin(pos, side).wait_recv()
        if crossing:
            added(out2.at[pos], [own_part(pos, side), recv1.at[pos * 2 + side]])
            to_pair(pos).start()

    turns = [(0, True)]
    for j in range(1, length):
        turns += [(j, True), (j - 1, False)]
    turns += [(length - 1, False)]

    def where(turn):
        return order(turn[0]), (1 - b if turn[1] else b)

    embed_sum[...] = jnp.zeros_like(embed_sum)
    for copy in fetches(0, *where(turns[0])):
        copy.start()
    greet(a, b, c, length, n_proto)
    ready = 0
    for q, turn in enumerate(turns):
        for copy in fetches(q, *where(turn)):
            copy.wait()
        if q + 1 < len(turns):
            for copy in fetches(q + 1, *where(turns[q + 1])):
                copy.start()
        make(q, *where(turn))
        to_twin(*where(turn)).start()
        if q + 1 == len(turns):
            for k in range(1, n_proto):
                to_peer(k).start()
        if q > 0:
            received(*turns[q - 1])
            if not turns[q - 1][1]:
                to_line(turns[q - 1][0])
    received(*turns[-1])
    embed_in[me] = embed_sum[...]
    for k in range(1, n_proto):
        to_peer(k).wait_recv()
    embeds[index_of(a, b, c)] = functools.reduce(jnp.add, [embed_in[k] for k in range(n_proto)]).astype(BF16)

    to_pair(a).wait_recv()
    final = own_part(a, b)

    @pl.when(a > 0)
    def _():
        to_right(a).wait_recv()

    @pl.when(a < length - 1)
    def _():
        to_left(a).wait_recv()

    @pl.when(a == 0)
    def _():
        added(final, terms(a) + [recv_r.at[a]])

    @pl.when(a == length - 1)
    def _():
        added(final, terms(a) + [recv_l.at[a]])

    @pl.when(jnp.logical_and(a > 0, a < length - 1))
    def _():
        added(final, terms(a) + [recv_l.at[a], recv_r.at[a]])

    done = pltpu.make_async_copy(final, out.at[index_of(a, b, c)], local)
    done.start()
    done.wait()
    gather_steps([(embeds, e_send, e_recv), (out, g_send, g_recv)], a, b, c, length)

    for pos in range(length):
        for side in range(2):
            to_twin(pos, side).wait_send()
        to_pair(pos).wait_send()

        @pl.when(pos > a)
        def _():
            to_right(pos).wait_send()

        @pl.when(pos < a)
        def _():
            to_left(pos).wait_send()

    for k in range(1, n_proto):
        to_peer(k).wait_send()


def reduce_call(n, n_proto, rows_in, tans, stats, anchors, moves, codes, collective_id):
    length = n // 4
    crops, width = rows_in.shape
    rows = anchors.shape[0] // n
    sems = pltpu.SemaphoreType.DMA
    block = lambda count: pltpu.VMEM((count, rows, width), BF16)
    near, far = pl.BlockSpec(memory_space=pltpu.VMEM), pl.BlockSpec(memory_space=pl.ANY)
    return pl.pallas_call(
        functools.partial(reduce_kernel, n, n_proto),
        out_shape=(
            jax.ShapeDtypeStruct((n, rows, width), BF16),
            jax.ShapeDtypeStruct((n, crops, width), BF16),
        ),
        in_specs=[near, near, near, far, far, far],
        out_specs=[far, near],
        scratch_shapes=[
            pltpu.VMEM((2, 2, rows, width), BF16), pltpu.VMEM((2, 2, rows, width), BF16),
            pltpu.VMEM((2, 2, crops, rows), BF16),
            block(n), block(2 * length), block(length), block(length), block(length),
            block(length), block(length), block(length),
            pltpu.VMEM((crops, width), F32), pltpu.VMEM((n_proto, crops, width), F32),
            sems((2, 2, 3)), sems((2 * length,)), sems((2 * length,)), sems((length,)), sems((length,)),
            sems((length,)), sems((length,)), sems((length,)), sems((length,)),
            sems((n_proto,)), sems((n_proto,)), sems,
            sems((4, n)), sems((n,)), sems((4, n)), sems((n,)),
        ],
        compiler_params=pltpu.CompilerParams(
            collective_id=collective_id, has_side_effects=True, vmem_limit_bytes=58 * MIB
        ),
    )(rows_in, tans, stats, anchors, moves, codes)


def dot_t(left, right):
    return lax.dot_general(left, right, (((1,), (1,)), ((), ())), preferred_element_type=F32)


def stats_kernel(rows_ref, tans_ref, a_ref, b_ref, codes_ref, out_ref, top, total, weighted, mass):
    i = pl.program_id(0)
    chunk = a_ref.shape[0]

    @pl.when(i == 0)
    def _():
        top[...] = jnp.full_like(top, -1e30)
        total[...] = jnp.zeros_like(total)
        weighted[...] = jnp.zeros_like(weighted)
        mass[...] = jnp.zeros_like(mass)

    left = jnp.concatenate([tans_ref[...], rows_ref[...]], axis=1)
    new, z, w, q = top[...], total[...], weighted[...], mass[...]
    part = math.gcd(chunk, 1024)
    for first in range(0, chunk, part):
        at = slice(first, first + part)
        s = dot_t(rows_ref[...], a_ref[at, :])
        tan = dot_t(left, jnp.concatenate([a_ref[at, :], b_ref[at, :]], axis=1))
        cols = [slice(k, k + LANES) for k in range(0, part, LANES)]
        old = new
        new = functools.reduce(jnp.maximum, [s[:, k] for k in cols], old)
        fade = jnp.exp2((old - new) * SCALE)
        z, w = z * fade, w * fade
        for k in cols:
            e = jnp.exp2((s[:, k] - new) * SCALE)
            z = z + e
            w = w + e * tan[:, k]
        for k in cols:
            q = q + codes_ref[:, first + k.start : first + k.stop].astype(F32)
    top[...], total[...], weighted[...], mass[...] = new, z, w, q

    @pl.when(i == pl.num_programs(0) - 1)
    def _():
        peak = jnp.max(top[...], axis=1, keepdims=True)
        scale = jnp.exp2((top[...] - peak) * SCALE)
        lane = lax.broadcasted_iota(jnp.int32, out_ref.shape, 1)
        values = [
            peak,
            jnp.sum(total[...] * scale, axis=1, keepdims=True),
            jnp.sum(weighted[...] * scale, axis=1, keepdims=True),
            jnp.sum(mass[...], axis=1, keepdims=True),
        ]
        out = jnp.zeros(out_ref.shape, F32)
        for k, v in enumerate(values):
            out = jnp.where(lane == k, v, out)
        out_ref[...] = out


def stats_call(rows, tans, anchors, moves, codes):
    crops, width = rows.shape
    protos = anchors.shape[0]
    chunk = math.gcd(protos, 2048)
    whole = pl.BlockSpec((crops, width), lambda i: (0, 0))
    block = pl.BlockSpec((chunk, width), lambda i: (i, 0))
    return pl.pallas_call(
        stats_kernel,
        grid=(protos // chunk,),
        out_shape=jax.ShapeDtypeStruct((crops, LANES), F32),
        in_specs=[whole, whole, block, block, pl.BlockSpec((crops, chunk), lambda i: (0, i))],
        out_specs=pl.BlockSpec((crops, LANES), lambda i: (0, 0)),
        scratch_shapes=[pltpu.VMEM((crops, LANES), F32)] * 4,
        compiler_params=pltpu.CompilerParams(vmem_limit_bytes=56 * MIB),
    )(rows, tans, anchors, moves, codes)


def weights(rows, tans, anchor, move, code, stats_ref):
    s = dot_t(rows, anchor)
    tan = dot_t(jnp.concatenate([tans, rows], axis=1), jnp.concatenate([anchor, move], axis=1))
    peak, gain, mean = stats_ref[:, 0:1], stats_ref[:, 1:2], stats_ref[:, 2:3]
    p = jnp.exp2((s - peak) * SCALE) * gain
    u = (p * (tan - mean)).astype(BF16)
    v = (TEMP * (p - code.astype(F32))).astype(BF16)
    embed = jnp.dot(u, anchor, preferred_element_type=F32) + jnp.dot(v, move, preferred_element_type=F32)
    part = lax.dot_general(
        jnp.concatenate([u, v], axis=0),
        jnp.concatenate([rows, tans], axis=0),
        (((0,), (0,)), ((), ())),
        preferred_element_type=F32,
    )
    return part.astype(BF16), embed


def body(n, n_proto, features, tangents, anchors, moves, codes, partner):
    crops, width = features.shape
    gathered = gather_call(n, jnp.concatenate([features, tangents], axis=1), 1)
    swapped = jnp.take(gathered.reshape(n * crops, 2 * width), partner, axis=0)
    rows, tans = swapped[:, :width], swapped[:, width:]
    local = stats_call(rows, tans, anchors, moves, codes)[:, :4].T
    mine = jnp.arange(n_proto) == lax.axis_index("proto")
    every = lax.psum(jnp.where(mine[:, None, None], local[None], 0.0), "proto")
    peak = jnp.max(every[:, 0], axis=0)
    scale = jnp.exp2((every[:, 0] - peak) * SCALE)
    total = jnp.sum(every[:, 1] * scale, axis=0)
    mean = jnp.sum(every[:, 2] * scale, axis=0) / total
    mass = jnp.sum(every[:, 3], axis=0)
    stats = jnp.stack([peak, mass / total, mean], axis=1)
    stats = jnp.pad(stats, ((0, 0), (0, LANES - 3)))
    protos = anchors.shape[0]
    out, embeds = reduce_call(n, n_proto, rows, tans, stats, anchors, moves, codes, 2)
    hvp_embed = jnp.take(embeds.reshape(n * crops, width), partner, axis=0)
    return hvp_embed, out.reshape(protos, width)


def solution(mesh):
    in_specs = (
        P("dp", None),
        P("dp", None),
        P("proto", None),
        P("proto", None),
        P("dp", "proto"),
        P("dp"),
    )
    out_specs = (P("dp", None), P("proto", None))
    return jax.shard_map(
        functools.partial(body, mesh.shape["dp"], mesh.shape["proto"]),
        mesh=mesh,
        in_specs=in_specs,
        out_specs=out_specs,
        check_vma=False,
    )
```

```python
import functools
import math

import jax
import jax.numpy as jnp
from jax import lax
from jax.experimental import pallas as pl
from jax.experimental.pallas import tpu as pltpu
from jax.sharding import PartitionSpec as P

MESH = pl.DeviceIdType.MESH
F32 = jnp.float32
BF16 = jnp.bfloat16
LOG2E = math.log2(math.e)
TEMP = 0.1
SCALE = LOG2E / TEMP
LANES = 128
MIB = 1024 * 1024


def place(n):
    d = lax.axis_index("dp")
    return d // 4, (d // 2) % 2, d % 2, n // 4


def index_of(a, b, c):
    return (a * 2 + b) * 2 + c


def greet(a, b, c, length, n_proto=1):
    barrier = pltpu.get_barrier_semaphore()

    def hello(target):
        pl.semaphore_signal(barrier, inc=1, device_id={"dp": target}, device_id_type=MESH)

    hello(index_of(a, b, 1 - c))
    hello(index_of(a, 1 - b, c))

    @pl.when(a > 0)
    def _():
        hello(index_of(a - 1, b, c))

    @pl.when(a < length - 1)
    def _():
        hello(index_of(a + 1, b, c))

    me = lax.axis_index("proto")
    for k in range(1, n_proto):
        pl.semaphore_signal(barrier, inc=1, device_id={"proto": (me + k) % n_proto}, device_id_type=MESH)
    peers = 1 + n_proto + jnp.where(a > 0, 1, 0) + jnp.where(a < length - 1, 1, 0)
    pl.semaphore_wait(barrier, peers)


class Copies:
    def __init__(self, arrays, block, kind, target):
        self.copies = [
            pltpu.make_async_remote_copy(
                src_ref=out.at[block, at],
                dst_ref=out.at[block, at],
                send_sem=send.at[kind, block],
                recv_sem=recv.at[block],
                device_id={"dp": target},
                device_id_type=MESH,
            )
            for out, send, recv, at in arrays
        ]

    def start(self):
        for copy in self.copies:
            copy.start()

    def wait_send(self):
        for copy in self.copies:
            copy.wait_send()

    def wait_recv(self):
        for copy in self.copies:
            copy.wait_recv()


def gather_steps(arrays, early, a, b, c, length):
    def copy(block, kind, target):
        return Copies(arrays, block, kind, target)

    def soon(block, kind, target):
        return Copies(early, block, kind, target)

    right, left = index_of(a + 1, b, c), index_of(a - 1, b, c)
    pair, twin = index_of(a, 1 - b, c), index_of(a, b, 1 - c)

    def line_block(pos):
        return index_of(pos, b, c)

    def spread(block, to_right, to_left):
        if to_right:

            @pl.when(a < length - 1)
            def _():
                copy(block, 0, right).start()

        if to_left:

            @pl.when(a > 0)
            def _():
                copy(block, 1, left).start()

        copy(block, 2, pair).start()
        copy(block, 3, twin).start()

    def spread_soon(block, to_right, to_left):
        if to_right:

            @pl.when(a < length - 1)
            def _():
                soon(block, 0, right).start()

        if to_left:

            @pl.when(a > 0)
            def _():
                soon(block, 1, left).start()

        soon(block, 3, twin).start()

    def from_pair(pos):
        block = index_of(pos, 1 - b, c)
        copy(block, 2, pair).wait_recv()
        copy(block, 3, twin).start()

    if early:
        soon(line_block(a), 2, pair).start()
    spread(line_block(a), True, True)
    if early:
        spread_soon(line_block(a), True, True)
        other = index_of(a, 1 - b, c)
        soon(other, 2, pair).wait_recv()
        spread_soon(other, True, True)
    for k in range(1, length):

        @pl.when(a - k >= 0)
        def _():
            copy(line_block(a - k), 0, right).wait_recv()
            spread(line_block(a - k), True, False)
            for side in (b, 1 - b) if early else ():
                soon(index_of(a - k, side, c), 0, right).wait_recv()
                spread_soon(index_of(a - k, side, c), True, False)

        @pl.when(a + k < length)
        def _():
            copy(line_block(a + k), 1, left).wait_recv()
            spread(line_block(a + k), False, True)
            for side in (b, 1 - b) if early else ():
                soon(index_of(a + k, side, c), 1, left).wait_recv()
                spread_soon(index_of(a + k, side, c), False, True)

    from_pair(a)
    for k in range(1, length):

        @pl.when(a - k >= 0)
        def _():
            from_pair(a - k)

        @pl.when(a + k < length)
        def _():
            from_pair(a + k)

    for pos in range(length):
        for side in range(2):
            copy(index_of(pos, side, 1 - c), 3, twin).wait_recv()
            if early:
                soon(index_of(pos, side, 1 - c), 3, twin).wait_recv()
    if early:
        soon(line_block(a), 2, pair).wait_send()
    for pos in range(length):
        copy(line_block(pos), 2, pair).wait_send()
        for side in range(2):
            copy(index_of(pos, side, c), 3, twin).wait_send()
            if early:
                soon(index_of(pos, side, c), 3, twin).wait_send()

        @pl.when(jnp.logical_and(a < length - 1, pos <= a))
        def _():
            copy(line_block(pos), 0, right).wait_send()
            for side in range(2) if early else ():
                soon(index_of(pos, side, c), 0, right).wait_send()

        @pl.when(jnp.logical_and(a > 0, pos >= a))
        def _():
            copy(line_block(pos), 1, left).wait_send()
            for side in range(2) if early else ():
                soon(index_of(pos, side, c), 1, left).wait_send()


def gather_kernel(n, x, y, out, send, recv, local):
    a, b, c, length = place(n)
    rows, width = x.shape
    mine = index_of(a, b, c)
    own = [
        pltpu.make_async_copy(part, out.at[mine, :, pl.ds(k * width, width)], local.at[k])
        for k, part in enumerate((x, y))
    ]
    for copy in own:
        copy.start()
    greet(a, b, c, length)
    for copy in own:
        copy.wait()
    gather_steps([(out, send, recv, pl.ds(0, rows))], [], a, b, c, length)


def gather_call(n, x, y, collective_id):
    rows, width = x.shape
    near = pl.BlockSpec(memory_space=pltpu.VMEM)
    return pl.pallas_call(
        functools.partial(gather_kernel, n),
        out_shape=jax.ShapeDtypeStruct((n, rows, 2 * width), x.dtype),
        in_specs=[near, near],
        out_specs=near,
        scratch_shapes=[
            pltpu.SemaphoreType.DMA((4, n)),
            pltpu.SemaphoreType.DMA((n,)),
            pltpu.SemaphoreType.DMA((2,)),
        ],
        compiler_params=pltpu.CompilerParams(
            collective_id=collective_id, has_side_effects=True, vmem_limit_bytes=56 * MIB
        ),
    )(x, y)


def reduce_kernel(n, n_proto, rows_ref, tans_ref, stats_ref, anchors, moves, codes, out, embeds,
                  a_buf, b_buf, c_buf, parts, recv1, recv2, recv_l, recv_r, out2, out_l, out_r, embed_sum, embed_in,
                  load, s1, r1, s2, r2, sl, sr, rl, rr, sx, rx, local, g_send, g_recv, h_send, h_recv, e_send, e_recv,
                  stats, stats_in, st, rt):
    a, b, c, length = place(n)
    me = lax.axis_index("proto")
    rows = parts.shape[1]
    step = math.gcd(rows, 256)
    tile = math.gcd(rows, 1024)
    tiles = rows // tile
    right, left = index_of(a + 1, b, c), index_of(a - 1, b, c)
    pair, twin = index_of(a, 1 - b, c), index_of(a, b, 1 - c)

    def order(j):
        return jnp.where(a < length // 2, (a - 1 - j + 2 * length) % length, (a + 1 + j) % length)

    def remote(src, dst, send, recv, target):
        return pltpu.make_async_remote_copy(
            src_ref=src, dst_ref=dst, send_sem=send, recv_sem=recv, device_id={"dp": target}, device_id_type=MESH
        )

    def to_twin(pos, side):
        k = pos * 2 + side
        return remote(parts.at[k * 2], recv1.at[k], s1.at[k], r1.at[k], twin)

    def own_part(pos, side):
        return parts.at[(pos * 2 + side) * 2 + 1]

    def to_peer(k):
        return pltpu.make_async_remote_copy(
            src_ref=embed_sum,
            dst_ref=embed_in.at[me],
            send_sem=sx.at[k],
            recv_sem=rx.at[k],
            device_id={"proto": (me + k) % n_proto},
            device_id_type=MESH,
        )

    def stats_to(k):
        return pltpu.make_async_remote_copy(
            src_ref=stats_ref,
            dst_ref=stats_in.at[me],
            send_sem=st.at[k],
            recv_sem=rt.at[k],
            device_id={"proto": (me + k) % n_proto},
            device_id_type=MESH,
        )

    def join_stats():
        every = [stats_in[k] for k in range(n_proto)]
        peak = functools.reduce(jnp.maximum, [x[:, 0:1] for x in every])
        scale = [jnp.exp2((x[:, 0:1] - peak) * SCALE) for x in every]
        total = functools.reduce(jnp.add, [x[:, 1:2] * f for x, f in zip(every, scale)])
        tangent = functools.reduce(jnp.add, [x[:, 2:3] * f for x, f in zip(every, scale)])
        mass = functools.reduce(jnp.add, [x[:, 3:4] for x in every])
        lane = lax.broadcasted_iota(jnp.int32, stats.shape, 1)
        stats[...] = jnp.where(lane == 0, peak, jnp.where(lane == 1, mass / total, tangent / total))

    def fetches(q, pos, side):
        slot = q % 2
        copies = []
        for w, core in enumerate((1 - c, c)):
            at = pl.ds(pl.multiple_of(index_of(pos, side, core) * rows, rows), rows)
            copies += [
                pltpu.make_async_copy(anchors.at[at, :], a_buf.at[slot, w], load.at[slot, w, 0]),
                pltpu.make_async_copy(moves.at[at, :], b_buf.at[slot, w], load.at[slot, w, 1]),
                pltpu.make_async_copy(codes.at[:, at], c_buf.at[slot, w], load.at[slot, w, 2]),
            ]
        return copies

    def make(q, pos, side):
        slot = q % 2

        def one(i, carry):
            w, at = i // tiles, pl.ds(pl.multiple_of((i % tiles) * tile, tile), tile)
            anchor, move, code = a_buf[slot, w, at, :], b_buf[slot, w, at, :], c_buf[slot, w, :, at]
            part, embed = weights(rows_ref[...], tans_ref[...], anchor, move, code, stats)
            parts[(pos * 2 + side) * 2 + w, at, :] = part
            embed_sum[...] += embed
            return carry

        lax.fori_loop(0, 2 * tiles, one, 0)

    def to_pair(pos):
        return remote(out2.at[pos], recv2.at[pos], s2.at[pos], r2.at[pos], pair)

    def to_right(pos):
        return remote(out_r.at[pos], recv_l.at[pos], sr.at[pos], rl.at[pos], right)

    def to_left(pos):
        return remote(out_l.at[pos], recv_r.at[pos], sl.at[pos], rr.at[pos], left)

    def added(dst, srcs):
        def one(i, carry):
            at = pl.ds(pl.multiple_of(i * step, step), step)
            total = srcs[0][at, :].astype(F32)
            for src in srcs[1:]:
                total = total + src[at, :].astype(F32)
            dst[at, :] = total.astype(dst.dtype)
            return carry

        lax.fori_loop(0, rows // step, one, 0)

    def terms(pos):
        return [own_part(pos, b), recv1.at[pos * 2 + b], recv2.at[pos]]

    def to_line(t):
        r_pos = length - 1 - (t - a)
        l_pos = t - (length - 1 - a)

        @pl.when(jnp.logical_and(t - a >= 0, r_pos > a))
        def _():
            to_pair(r_pos).wait_recv()

            @pl.when(a > 0)
            def _():
                to_right(r_pos).wait_recv()
                added(out_r.at[r_pos], terms(r_pos) + [recv_l.at[r_pos]])

            @pl.when(a == 0)
            def _():
                added(out_r.at[r_pos], terms(r_pos))

            to_right(r_pos).start()

        @pl.when(jnp.logical_and(l_pos >= 0, l_pos < a))
        def _():
            to_pair(l_pos).wait_recv()

            @pl.when(a < length - 1)
            def _():
                to_left(l_pos).wait_recv()
                added(out_l.at[l_pos], terms(l_pos) + [recv_r.at[l_pos]])

            @pl.when(a == length - 1)
            def _():
                added(out_l.at[l_pos], terms(l_pos))

            to_left(l_pos).start()

    def received(j, crossing):
        pos = order(j)
        side = 1 - b if crossing else b
        to_twin(pos, side).wait_recv()
        if crossing:
            added(out2.at[pos], [own_part(pos, side), recv1.at[pos * 2 + side]])
            to_pair(pos).start()

    turns = [(0, True)]
    for j in range(1, length):
        turns += [(j, True), (j - 1, False)]
    turns += [(length - 1, False)]

    def where(turn):
        return order(turn[0]), (1 - b if turn[1] else b)

    embed_sum[...] = jnp.zeros_like(embed_sum)
    for copy in fetches(0, *where(turns[0])):
        copy.start()
    greet(a, b, c, length, n_proto)
    for k in range(1, n_proto):
        stats_to(k).start()
    stats_in[me] = stats_ref[...]
    for k in range(1, n_proto):
        stats_to(k).wait_recv()
    join_stats()
    for q, turn in enumerate(turns):
        for copy in fetches(q, *where(turn)):
            copy.wait()
        if q + 1 < len(turns):
            for copy in fetches(q + 1, *where(turns[q + 1])):
                copy.start()
        make(q, *where(turn))
        to_twin(*where(turn)).start()
        if q + 1 == len(turns):
            for k in range(1, n_proto):
                to_peer(k).start()
        if q > 0:
            received(*turns[q - 1])
            if not turns[q - 1][1]:
                to_line(turns[q - 1][0])
    received(*turns[-1])
    embed_in[me] = embed_sum[...]
    for k in range(1, n_proto):
        to_peer(k).wait_recv()
    embeds[index_of(a, b, c)] = functools.reduce(jnp.add, [embed_in[k] for k in range(n_proto)]).astype(BF16)

    to_pair(a).wait_recv()
    final = own_part(a, b)

    @pl.when(a > 0)
    def _():
        to_right(a).wait_recv()

    @pl.when(a < length - 1)
    def _():
        to_left(a).wait_recv()

    @pl.when(a == 0)
    def _():
        added(final, terms(a) + [recv_r.at[a]])

    @pl.when(a == length - 1)
    def _():
        added(final, terms(a) + [recv_l.at[a]])

    @pl.when(jnp.logical_and(a > 0, a < length - 1))
    def _():
        added(final, terms(a) + [recv_l.at[a], recv_r.at[a]])

    done = pltpu.make_async_copy(final, out.at[index_of(a, b, c)], local)
    done.start()
    done.wait()
    crops = embeds.shape[1]
    cut = rows // 8
    whole = [(embeds, e_send, e_recv, pl.ds(0, crops)), (out, g_send, g_recv, pl.ds(cut, rows - cut))]
    gather_steps(whole, [(out, h_send, h_recv, pl.ds(0, cut))], a, b, c, length)

    for pos in range(length):
        for side in range(2):
            to_twin(pos, side).wait_send()
        to_pair(pos).wait_send()

        @pl.when(pos > a)
        def _():
            to_right(pos).wait_send()

        @pl.when(pos < a)
        def _():
            to_left(pos).wait_send()

    for k in range(1, n_proto):
        to_peer(k).wait_send()
        stats_to(k).wait_send()


def reduce_call(n, n_proto, rows_in, tans, stats, anchors, moves, codes, collective_id):
    length = n // 4
    crops, width = rows_in.shape
    rows = anchors.shape[0] // n
    sems = pltpu.SemaphoreType.DMA
    block = lambda count: pltpu.VMEM((count, rows, width), BF16)
    near, far = pl.BlockSpec(memory_space=pltpu.VMEM), pl.BlockSpec(memory_space=pl.ANY)
    return pl.pallas_call(
        functools.partial(reduce_kernel, n, n_proto),
        out_shape=(
            jax.ShapeDtypeStruct((n, rows, width), BF16),
            jax.ShapeDtypeStruct((n, crops, width), BF16),
        ),
        in_specs=[near, near, near, far, far, far],
        out_specs=[far, near],
        scratch_shapes=[
            pltpu.VMEM((2, 2, rows, width), BF16), pltpu.VMEM((2, 2, rows, width), BF16),
            pltpu.VMEM((2, 2, crops, rows), BF16),
            block(n), block(2 * length), block(length), block(length), block(length),
            block(length), block(length), block(length),
            pltpu.VMEM((crops, width), F32), pltpu.VMEM((n_proto, crops, width), F32),
            sems((2, 2, 3)), sems((2 * length,)), sems((2 * length,)), sems((length,)), sems((length,)),
            sems((length,)), sems((length,)), sems((length,)), sems((length,)),
            sems((n_proto,)), sems((n_proto,)), sems,
            sems((4, n)), sems((n,)), sems((4, n)), sems((n,)), sems((4, n)), sems((n,)),
            pltpu.VMEM((crops, LANES), F32), pltpu.VMEM((n_proto, crops, LANES), F32),
            sems((n_proto,)), sems((n_proto,)),
        ],
        compiler_params=pltpu.CompilerParams(
            collective_id=collective_id, has_side_effects=True, vmem_limit_bytes=58 * MIB
        ),
    )(rows_in, tans, stats, anchors, moves, codes)


def dot_t(left, right):
    return lax.dot_general(left, right, (((1,), (1,)), ((), ())), preferred_element_type=F32)


def products(rows, tans, anchor, move):
    crops = rows.shape[0]
    upper = jnp.concatenate([rows, jnp.zeros_like(rows)], axis=1)
    lower = jnp.concatenate([tans, rows], axis=1)
    both = dot_t(jnp.concatenate([upper, lower], axis=0), jnp.concatenate([anchor, move], axis=1))
    return both[:crops], both[crops:]


def stats_kernel(rows_ref, tans_ref, a_ref, b_ref, codes_ref, out_ref, top, total, weighted, mass):
    i = pl.program_id(0)
    chunk = a_ref.shape[0]

    @pl.when(i == 0)
    def _():
        top[...] = jnp.full_like(top, -1e30)
        total[...] = jnp.zeros_like(total)
        weighted[...] = jnp.zeros_like(weighted)
        mass[...] = jnp.zeros_like(mass)

    new, z, w, q = top[...], total[...], weighted[...], mass[...]
    part = math.gcd(chunk, 1024)
    for first in range(0, chunk, part):
        at = slice(first, first + part)
        s, tan = products(rows_ref[...], tans_ref[...], a_ref[at, :], b_ref[at, :])
        cols = [slice(k, k + LANES) for k in range(0, part, LANES)]
        old = new
        new = functools.reduce(jnp.maximum, [s[:, k] for k in cols], old)
        fade = jnp.exp2((old - new) * SCALE)
        z, w = z * fade, w * fade
        for k in cols:
            e = jnp.exp2((s[:, k] - new) * SCALE)
            z = z + e
            w = w + e * tan[:, k]
        for k in cols:
            q = q + codes_ref[:, first + k.start : first + k.stop].astype(F32)
    top[...], total[...], weighted[...], mass[...] = new, z, w, q

    @pl.when(i == pl.num_programs(0) - 1)
    def _():
        peak = jnp.max(top[...], axis=1, keepdims=True)
        scale = jnp.exp2((top[...] - peak) * SCALE)
        lane = lax.broadcasted_iota(jnp.int32, out_ref.shape, 1)
        values = [
            peak,
            jnp.sum(total[...] * scale, axis=1, keepdims=True),
            jnp.sum(weighted[...] * scale, axis=1, keepdims=True),
            jnp.sum(mass[...], axis=1, keepdims=True),
        ]
        out = jnp.zeros(out_ref.shape, F32)
        for k, v in enumerate(values):
            out = jnp.where(lane == k, v, out)
        out_ref[...] = out


def stats_call(rows, tans, anchors, moves, codes):
    crops, width = rows.shape
    protos = anchors.shape[0]
    chunk = math.gcd(protos, 2048)
    whole = pl.BlockSpec((crops, width), lambda i: (0, 0))
    block = pl.BlockSpec((chunk, width), lambda i: (i, 0))
    return pl.pallas_call(
        stats_kernel,
        grid=(protos // chunk,),
        out_shape=jax.ShapeDtypeStruct((crops, LANES), F32),
        in_specs=[whole, whole, block, block, pl.BlockSpec((crops, chunk), lambda i: (0, i))],
        out_specs=pl.BlockSpec((crops, LANES), lambda i: (0, 0)),
        scratch_shapes=[pltpu.VMEM((crops, LANES), F32)] * 4,
        compiler_params=pltpu.CompilerParams(vmem_limit_bytes=56 * MIB),
    )(rows, tans, anchors, moves, codes)


def weights(rows, tans, anchor, move, code, stats_ref):
    s, tan = products(rows, tans, anchor, move)
    peak, gain, mean = stats_ref[:, 0:1], stats_ref[:, 1:2], stats_ref[:, 2:3]
    p = jnp.exp2((s - peak) * SCALE) * gain
    u = (p * (tan - mean)).astype(BF16)
    v = (TEMP * (p - code.astype(F32))).astype(BF16)
    embed = jnp.dot(u, anchor, preferred_element_type=F32) + jnp.dot(v, move, preferred_element_type=F32)
    part = lax.dot_general(
        jnp.concatenate([u, v], axis=0),
        jnp.concatenate([rows, tans], axis=0),
        (((0,), (0,)), ((), ())),
        preferred_element_type=F32,
    )
    return part.astype(BF16), embed


def body(n, n_proto, features, tangents, anchors, moves, codes, partner):
    crops, width = features.shape
    protos = anchors.shape[0]
    gathered = gather_call(n, features, tangents, 1)
    swapped = gathered.reshape(n * crops, 2 * width).at[partner].get(mode="promise_in_bounds")
    rows, tans = swapped[:, :width], swapped[:, width:]
    local = stats_call(rows, tans, anchors, moves, codes)
    out, embeds = reduce_call(n, n_proto, rows, tans, local, anchors, moves, codes, 2)
    hvp_embed = embeds.reshape(n * crops, width).at[partner].get(mode="promise_in_bounds")
    return hvp_embed, out.reshape(protos, width)


def solution(mesh):
    in_specs = (
        P("dp", None),
        P("dp", None),
        P("proto", None),
        P("proto", None),
        P("dp", "proto"),
        P("dp"),
    )
    out_specs = (P("dp", None), P("proto", None))
    return jax.shard_map(
        functools.partial(body, mesh.shape["dp"], mesh.shape["proto"]),
        mesh=mesh,
        in_specs=in_specs,
        out_specs=out_specs,
        check_vma=False,
    )
```

```python
import functools
import math

import jax
import jax.numpy as jnp
from jax import lax
from jax.experimental import pallas as pl
from jax.experimental.pallas import tpu as pltpu
from jax.sharding import PartitionSpec as P

MESH = pl.DeviceIdType.MESH
F32 = jnp.float32
BF16 = jnp.bfloat16
LOG2E = math.log2(math.e)
TEMP = 0.1
SCALE = LOG2E / TEMP
LANES = 128
MIB = 1024 * 1024


def place(n):
    d = lax.axis_index("dp")
    return d // 4, (d // 2) % 2, d % 2, n // 4


def index_of(a, b, c):
    return (a * 2 + b) * 2 + c


def greet(a, b, c, length, n_proto=1):
    barrier = pltpu.get_barrier_semaphore()

    def hello(target):
        pl.semaphore_signal(barrier, inc=1, device_id={"dp": target}, device_id_type=MESH)

    hello(index_of(a, b, 1 - c))
    hello(index_of(a, 1 - b, c))

    @pl.when(a > 0)
    def _():
        hello(index_of(a - 1, b, c))

    @pl.when(a < length - 1)
    def _():
        hello(index_of(a + 1, b, c))

    me = lax.axis_index("proto")
    for k in range(1, n_proto):
        pl.semaphore_signal(barrier, inc=1, device_id={"proto": (me + k) % n_proto}, device_id_type=MESH)
    peers = 1 + n_proto + jnp.where(a > 0, 1, 0) + jnp.where(a < length - 1, 1, 0)
    pl.semaphore_wait(barrier, peers)


class Copies:
    def __init__(self, arrays, block, kind, target):
        self.copies = [
            pltpu.make_async_remote_copy(
                src_ref=out.at[block, at],
                dst_ref=out.at[block, at],
                send_sem=send.at[kind, block],
                recv_sem=recv.at[block],
                device_id={"dp": target},
                device_id_type=MESH,
            )
            for out, send, recv, at in arrays
        ]

    def start(self):
        for copy in self.copies:
            copy.start()

    def wait_send(self):
        for copy in self.copies:
            copy.wait_send()

    def wait_recv(self):
        for copy in self.copies:
            copy.wait_recv()


def gather_steps(arrays, early, a, b, c, length):
    def copy(block, kind, target):
        return Copies(arrays, block, kind, target)

    def soon(block, kind, target):
        return Copies(early, block, kind, target)

    right, left = index_of(a + 1, b, c), index_of(a - 1, b, c)
    pair, twin = index_of(a, 1 - b, c), index_of(a, b, 1 - c)

    def line_block(pos):
        return index_of(pos, b, c)

    def spread(block, to_right, to_left):
        if to_right:

            @pl.when(a < length - 1)
            def _():
                copy(block, 0, right).start()

        if to_left:

            @pl.when(a > 0)
            def _():
                copy(block, 1, left).start()

        copy(block, 2, pair).start()
        copy(block, 3, twin).start()

    def spread_soon(block, to_right, to_left):
        if to_right:

            @pl.when(a < length - 1)
            def _():
                soon(block, 0, right).start()

        if to_left:

            @pl.when(a > 0)
            def _():
                soon(block, 1, left).start()

        soon(block, 3, twin).start()

    def from_pair(pos):
        block = index_of(pos, 1 - b, c)
        copy(block, 2, pair).wait_recv()
        copy(block, 3, twin).start()

    if early:
        soon(line_block(a), 2, pair).start()
    spread(line_block(a), True, True)
    if early:
        spread_soon(line_block(a), True, True)
        other = index_of(a, 1 - b, c)
        soon(other, 2, pair).wait_recv()
        spread_soon(other, True, True)
    for k in range(1, length):

        @pl.when(a - k >= 0)
        def _():
            copy(line_block(a - k), 0, right).wait_recv()
            spread(line_block(a - k), True, False)
            for side in (b, 1 - b) if early else ():
                soon(index_of(a - k, side, c), 0, right).wait_recv()
                spread_soon(index_of(a - k, side, c), True, False)

        @pl.when(a + k < length)
        def _():
            copy(line_block(a + k), 1, left).wait_recv()
            spread(line_block(a + k), False, True)
            for side in (b, 1 - b) if early else ():
                soon(index_of(a + k, side, c), 1, left).wait_recv()
                spread_soon(index_of(a + k, side, c), False, True)

    from_pair(a)
    for k in range(1, length):

        @pl.when(a - k >= 0)
        def _():
            from_pair(a - k)

        @pl.when(a + k < length)
        def _():
            from_pair(a + k)

    for pos in range(length):
        for side in range(2):
            copy(index_of(pos, side, 1 - c), 3, twin).wait_recv()
            if early:
                soon(index_of(pos, side, 1 - c), 3, twin).wait_recv()
    if early:
        soon(line_block(a), 2, pair).wait_send()
    for pos in range(length):
        copy(line_block(pos), 2, pair).wait_send()
        for side in range(2):
            copy(index_of(pos, side, c), 3, twin).wait_send()
            if early:
                soon(index_of(pos, side, c), 3, twin).wait_send()

        @pl.when(jnp.logical_and(a < length - 1, pos <= a))
        def _():
            copy(line_block(pos), 0, right).wait_send()
            for side in range(2) if early else ():
                soon(index_of(pos, side, c), 0, right).wait_send()

        @pl.when(jnp.logical_and(a > 0, pos >= a))
        def _():
            copy(line_block(pos), 1, left).wait_send()
            for side in range(2) if early else ():
                soon(index_of(pos, side, c), 1, left).wait_send()


def gather_kernel(n, x, y, out, send, recv, local):
    a, b, c, length = place(n)
    rows, width = x.shape
    mine = index_of(a, b, c)
    own = [
        pltpu.make_async_copy(part, out.at[mine, :, pl.ds(k * width, width)], local.at[k])
        for k, part in enumerate((x, y))
    ]
    for copy in own:
        copy.start()
    greet(a, b, c, length)
    for copy in own:
        copy.wait()
    gather_steps([(out, send, recv, pl.ds(0, rows))], [], a, b, c, length)


def gather_call(n, x, y, collective_id):
    rows, width = x.shape
    near = pl.BlockSpec(memory_space=pltpu.VMEM)
    return pl.pallas_call(
        functools.partial(gather_kernel, n),
        out_shape=jax.ShapeDtypeStruct((n, rows, 2 * width), x.dtype),
        in_specs=[near, near],
        out_specs=near,
        scratch_shapes=[
            pltpu.SemaphoreType.DMA((4, n)),
            pltpu.SemaphoreType.DMA((n,)),
            pltpu.SemaphoreType.DMA((2,)),
        ],
        compiler_params=pltpu.CompilerParams(
            collective_id=collective_id, has_side_effects=True, vmem_limit_bytes=56 * MIB
        ),
    )(x, y)


def reduce_kernel(n, n_proto, rows_ref, tans_ref, stats_ref, anchors, moves, codes, out, embeds,
                  a_buf, b_buf, c_buf, parts, recv1, recv2, recv_l, recv_r, out2, out_l, out_r, embed_sum, embed_in,
                  load, s1, r1, s2, r2, sl, sr, rl, rr, sx, rx, local, g_send, g_recv, h_send, h_recv, e_send, e_recv,
                  stats, stats_in, st, rt):
    a, b, c, length = place(n)
    me = lax.axis_index("proto")
    rows = parts.shape[1]
    step = math.gcd(rows, 256)
    tile = math.gcd(rows, 1024)
    tiles = rows // tile
    right, left = index_of(a + 1, b, c), index_of(a - 1, b, c)
    pair, twin = index_of(a, 1 - b, c), index_of(a, b, 1 - c)

    def order(j):
        return jnp.where(a < length // 2, (a - 1 - j + 2 * length) % length, (a + 1 + j) % length)

    def remote(src, dst, send, recv, target):
        return pltpu.make_async_remote_copy(
            src_ref=src, dst_ref=dst, send_sem=send, recv_sem=recv, device_id={"dp": target}, device_id_type=MESH
        )

    def to_twin(pos, side):
        k = pos * 2 + side
        return remote(parts.at[k * 2], recv1.at[k], s1.at[k], r1.at[k], twin)

    def own_part(pos, side):
        return parts.at[(pos * 2 + side) * 2 + 1]

    def to_peer(k):
        return pltpu.make_async_remote_copy(
            src_ref=embed_sum,
            dst_ref=embed_in.at[me],
            send_sem=sx.at[k],
            recv_sem=rx.at[k],
            device_id={"proto": (me + k) % n_proto},
            device_id_type=MESH,
        )

    def stats_to(k):
        return pltpu.make_async_remote_copy(
            src_ref=stats_ref,
            dst_ref=stats_in.at[me],
            send_sem=st.at[k],
            recv_sem=rt.at[k],
            device_id={"proto": (me + k) % n_proto},
            device_id_type=MESH,
        )

    def join_stats():
        every = [stats_in[k] for k in range(n_proto)]
        peak = functools.reduce(jnp.maximum, [x[:, 0:1] for x in every])
        scale = [jnp.exp2((x[:, 0:1] - peak) * SCALE) for x in every]
        total = functools.reduce(jnp.add, [x[:, 1:2] * f for x, f in zip(every, scale)])
        tangent = functools.reduce(jnp.add, [x[:, 2:3] * f for x, f in zip(every, scale)])
        mass = functools.reduce(jnp.add, [x[:, 3:4] for x in every])
        lane = lax.broadcasted_iota(jnp.int32, stats.shape, 1)
        stats[...] = jnp.where(lane == 0, peak, jnp.where(lane == 1, mass / total, tangent / total))

    def fetches(q, pos, side):
        slot = q % 2
        copies = []
        for w, core in enumerate((1 - c, c)):
            at = pl.ds(pl.multiple_of(index_of(pos, side, core) * rows, rows), rows)
            copies += [
                pltpu.make_async_copy(anchors.at[at, :], a_buf.at[slot, w], load.at[slot, w, 0]),
                pltpu.make_async_copy(moves.at[at, :], b_buf.at[slot, w], load.at[slot, w, 1]),
                pltpu.make_async_copy(codes.at[:, at], c_buf.at[slot, w], load.at[slot, w, 2]),
            ]
        return copies

    def make(q, pos, side):
        slot = q % 2

        def one(i, carry):
            w, at = i // tiles, pl.ds(pl.multiple_of((i % tiles) * tile, tile), tile)
            anchor, move, code = a_buf[slot, w, at, :], b_buf[slot, w, at, :], c_buf[slot, w, :, at]
            part, embed = weights(rows_ref[...], tans_ref[...], anchor, move, code, stats)
            parts[(pos * 2 + side) * 2 + w, at, :] = part
            embed_sum[...] += embed
            return carry

        lax.fori_loop(0, 2 * tiles, one, 0)

    def to_pair(pos):
        return remote(out2.at[pos], recv2.at[pos], s2.at[pos], r2.at[pos], pair)

    def to_right(pos):
        return remote(out_r.at[pos], recv_l.at[pos], sr.at[pos], rl.at[pos], right)

    def to_left(pos):
        return remote(out_l.at[pos], recv_r.at[pos], sl.at[pos], rr.at[pos], left)

    def added(dst, srcs):
        def one(i, carry):
            at = pl.ds(pl.multiple_of(i * step, step), step)
            total = srcs[0][at, :].astype(F32)
            for src in srcs[1:]:
                total = total + src[at, :].astype(F32)
            dst[at, :] = total.astype(dst.dtype)
            return carry

        lax.fori_loop(0, rows // step, one, 0)

    def terms(pos):
        return [own_part(pos, b), recv1.at[pos * 2 + b], recv2.at[pos]]

    def to_line(t):
        r_pos = length - 1 - (t - a)
        l_pos = t - (length - 1 - a)

        @pl.when(jnp.logical_and(t - a >= 0, r_pos > a))
        def _():
            to_pair(r_pos).wait_recv()

            @pl.when(a > 0)
            def _():
                to_right(r_pos).wait_recv()
                added(out_r.at[r_pos], terms(r_pos) + [recv_l.at[r_pos]])

            @pl.when(a == 0)
            def _():
                added(out_r.at[r_pos], terms(r_pos))

            to_right(r_pos).start()

        @pl.when(jnp.logical_and(l_pos >= 0, l_pos < a))
        def _():
            to_pair(l_pos).wait_recv()

            @pl.when(a < length - 1)
            def _():
                to_left(l_pos).wait_recv()
                added(out_l.at[l_pos], terms(l_pos) + [recv_r.at[l_pos]])

            @pl.when(a == length - 1)
            def _():
                added(out_l.at[l_pos], terms(l_pos))

            to_left(l_pos).start()

    def received(j, crossing):
        pos = order(j)
        side = 1 - b if crossing else b
        to_twin(pos, side).wait_recv()
        if crossing:
            added(out2.at[pos], [own_part(pos, side), recv1.at[pos * 2 + side]])
            to_pair(pos).start()

    turns = [(0, True)]
    for j in range(1, length):
        turns += [(j, True), (j - 1, False)]
    turns += [(length - 1, False)]

    def where(turn):
        return order(turn[0]), (1 - b if turn[1] else b)

    embed_sum[...] = jnp.zeros_like(embed_sum)
    for copy in fetches(0, *where(turns[0])):
        copy.start()
    greet(a, b, c, length, n_proto)
    for k in range(1, n_proto):
        stats_to(k).start()
    stats_in[me] = stats_ref[...]
    for k in range(1, n_proto):
        stats_to(k).wait_recv()
    join_stats()
    for q, turn in enumerate(turns):
        for copy in fetches(q, *where(turn)):
            copy.wait()
        if q + 1 < len(turns):
            for copy in fetches(q + 1, *where(turns[q + 1])):
                copy.start()
        make(q, *where(turn))
        to_twin(*where(turn)).start()
        if q + 1 == len(turns):
            for k in range(1, n_proto):
                to_peer(k).start()
        if q > 0:
            received(*turns[q - 1])
            if not turns[q - 1][1]:
                to_line(turns[q - 1][0])
    received(*turns[-1])
    embed_in[me] = embed_sum[...]
    for k in range(1, n_proto):
        to_peer(k).wait_recv()
    embeds[index_of(a, b, c)] = functools.reduce(jnp.add, [embed_in[k] for k in range(n_proto)]).astype(BF16)

    to_pair(a).wait_recv()
    final = own_part(a, b)

    @pl.when(a > 0)
    def _():
        to_right(a).wait_recv()

    @pl.when(a < length - 1)
    def _():
        to_left(a).wait_recv()

    @pl.when(a == 0)
    def _():
        added(final, terms(a) + [recv_r.at[a]])

    @pl.when(a == length - 1)
    def _():
        added(final, terms(a) + [recv_l.at[a]])

    @pl.when(jnp.logical_and(a > 0, a < length - 1))
    def _():
        added(final, terms(a) + [recv_l.at[a], recv_r.at[a]])

    done = pltpu.make_async_copy(final, out.at[index_of(a, b, c)], local)
    done.start()
    done.wait()
    crops = embeds.shape[1]
    cut = rows // 8
    whole = [(embeds, e_send, e_recv, pl.ds(0, crops)), (out, g_send, g_recv, pl.ds(cut, rows - cut))]
    gather_steps(whole, [(out, h_send, h_recv, pl.ds(0, cut))], a, b, c, length)

    for pos in range(length):
        for side in range(2):
            to_twin(pos, side).wait_send()
        to_pair(pos).wait_send()

        @pl.when(pos > a)
        def _():
            to_right(pos).wait_send()

        @pl.when(pos < a)
        def _():
            to_left(pos).wait_send()

    for k in range(1, n_proto):
        to_peer(k).wait_send()
        stats_to(k).wait_send()


def reduce_call(n, n_proto, rows_in, tans, stats, anchors, moves, codes, collective_id):
    length = n // 4
    crops, width = rows_in.shape
    rows = anchors.shape[0] // n
    sems = pltpu.SemaphoreType.DMA
    block = lambda count: pltpu.VMEM((count, rows, width), BF16)
    near, far = pl.BlockSpec(memory_space=pltpu.VMEM), pl.BlockSpec(memory_space=pl.ANY)
    return pl.pallas_call(
        functools.partial(reduce_kernel, n, n_proto),
        out_shape=(
            jax.ShapeDtypeStruct((n, rows, width), BF16),
            jax.ShapeDtypeStruct((n, crops, width), BF16),
        ),
        in_specs=[near, near, near, far, far, far],
        out_specs=[far, near],
        scratch_shapes=[
            pltpu.VMEM((2, 2, rows, width), BF16), pltpu.VMEM((2, 2, rows, width), BF16),
            pltpu.VMEM((2, 2, crops, rows), BF16),
            block(n), block(2 * length), block(length), block(length), block(length),
            block(length), block(length), block(length),
            pltpu.VMEM((crops, width), F32), pltpu.VMEM((n_proto, crops, width), F32),
            sems((2, 2, 3)), sems((2 * length,)), sems((2 * length,)), sems((length,)), sems((length,)),
            sems((length,)), sems((length,)), sems((length,)), sems((length,)),
            sems((n_proto,)), sems((n_proto,)), sems,
            sems((4, n)), sems((n,)), sems((4, n)), sems((n,)), sems((4, n)), sems((n,)),
            pltpu.VMEM((crops, LANES), F32), pltpu.VMEM((n_proto, crops, LANES), F32),
            sems((n_proto,)), sems((n_proto,)),
        ],
        compiler_params=pltpu.CompilerParams(
            collective_id=collective_id, has_side_effects=True, vmem_limit_bytes=58 * MIB
        ),
    )(rows_in, tans, stats, anchors, moves, codes)


def dot_t(left, right):
    return lax.dot_general(left, right, (((1,), (1,)), ((), ())), preferred_element_type=F32)


def products(rows, tans, anchor, move):
    crops = rows.shape[0]
    upper = jnp.concatenate([rows, jnp.zeros_like(rows)], axis=1)
    lower = jnp.concatenate([tans, rows], axis=1)
    both = dot_t(jnp.concatenate([upper, lower], axis=0), jnp.concatenate([anchor, move], axis=1))
    return both[:crops], both[crops:]


def stats_kernel(rows_ref, tans_ref, a_ref, b_ref, codes_ref, out_ref, top, total, weighted, mass):
    i = pl.program_id(0)
    chunk = a_ref.shape[0]

    @pl.when(i == 0)
    def _():
        top[...] = jnp.full_like(top, -1e30)
        total[...] = jnp.zeros_like(total)
        weighted[...] = jnp.zeros_like(weighted)
        mass[...] = jnp.zeros_like(mass)

    new, z, w, q = top[...], total[...], weighted[...], mass[...]
    part = math.gcd(chunk, 1024)
    for first in range(0, chunk, part):
        at = slice(first, first + part)
        s, tan = products(rows_ref[...], tans_ref[...], a_ref[at, :], b_ref[at, :])
        cols = [slice(k, k + LANES) for k in range(0, part, LANES)]
        old = new
        new = functools.reduce(jnp.maximum, [s[:, k] for k in cols], old)
        fade = jnp.exp2((old - new) * SCALE)
        z, w = z * fade, w * fade
        for k in cols:
            e = jnp.exp2((s[:, k] - new) * SCALE)
            z = z + e
            w = w + e * tan[:, k]
        for k in cols:
            q = q + codes_ref[:, first + k.start : first + k.stop].astype(F32)
    top[...], total[...], weighted[...], mass[...] = new, z, w, q

    @pl.when(i == pl.num_programs(0) - 1)
    def _():
        peak = jnp.max(top[...], axis=1, keepdims=True)
        scale = jnp.exp2((top[...] - peak) * SCALE)
        lane = lax.broadcasted_iota(jnp.int32, out_ref.shape, 1)
        values = [
            peak,
            jnp.sum(total[...] * scale, axis=1, keepdims=True),
            jnp.sum(weighted[...] * scale, axis=1, keepdims=True),
            jnp.sum(mass[...], axis=1, keepdims=True),
        ]
        out = jnp.zeros(out_ref.shape, F32)
        for k, v in enumerate(values):
            out = jnp.where(lane == k, v, out)
        out_ref[...] = out


def stats_call(rows, tans, anchors, moves, codes):
    crops, width = rows.shape
    protos = anchors.shape[0]
    chunk = math.gcd(protos, 4096)
    whole = pl.BlockSpec((crops, width), lambda i: (0, 0))
    block = pl.BlockSpec((chunk, width), lambda i: (i, 0))
    return pl.pallas_call(
        stats_kernel,
        grid=(protos // chunk,),
        out_shape=jax.ShapeDtypeStruct((crops, LANES), F32),
        in_specs=[whole, whole, block, block, pl.BlockSpec((crops, chunk), lambda i: (0, i))],
        out_specs=pl.BlockSpec((crops, LANES), lambda i: (0, 0)),
        scratch_shapes=[pltpu.VMEM((crops, LANES), F32)] * 4,
        compiler_params=pltpu.CompilerParams(vmem_limit_bytes=56 * MIB),
    )(rows, tans, anchors, moves, codes)


def weights(rows, tans, anchor, move, code, stats_ref):
    s, tan = products(rows, tans, anchor, move)
    peak, gain, mean = stats_ref[:, 0:1], stats_ref[:, 1:2], stats_ref[:, 2:3]
    p = jnp.exp2((s - peak) * SCALE) * gain
    u = (p * (tan - mean)).astype(BF16)
    v = (TEMP * (p - code.astype(F32))).astype(BF16)
    embed = jnp.dot(u, anchor, preferred_element_type=F32) + jnp.dot(v, move, preferred_element_type=F32)
    part = lax.dot_general(
        jnp.concatenate([u, v], axis=0),
        jnp.concatenate([rows, tans], axis=0),
        (((0,), (0,)), ((), ())),
        preferred_element_type=F32,
    )
    return part.astype(BF16), embed


def body(n, n_proto, features, tangents, anchors, moves, codes, partner):
    crops, width = features.shape
    protos = anchors.shape[0]
    gathered = gather_call(n, features, tangents, 1)
    swapped = gathered.reshape(n * crops, 2 * width).at[partner].get(mode="promise_in_bounds")
    rows, tans = swapped[:, :width], swapped[:, width:]
    local = stats_call(rows, tans, anchors, moves, codes)
    out, embeds = reduce_call(n, n_proto, rows, tans, local, anchors, moves, codes, 2)
    hvp_embed = embeds.reshape(n * crops, width).at[partner].get(mode="promise_in_bounds")
    return hvp_embed, out.reshape(protos, width)


def solution(mesh):
    in_specs = (
        P("dp", None),
        P("dp", None),
        P("proto", None),
        P("proto", None),
        P("dp", "proto"),
        P("dp"),
    )
    out_specs = (P("dp", None), P("proto", None))
    return jax.shard_map(
        functools.partial(body, mesh.shape["dp"], mesh.shape["proto"]),
        mesh=mesh,
        in_specs=in_specs,
        out_specs=out_specs,
        check_vma=False,
    )
```
